32 devices in a mesh: docs: 2 (over y), seq: 4 (over z), head: 4 (over x, core).
Axes of the slice: x: 2, y: 2, z: 4, core: 2. Of those that a mesh axis runs over, the one named last changes fastest.
Arguments:
- tokens: bfloat16 [6144, 1024], P(('docs', 'seq'), 'head'), parts along dimension 0, may hold values from -6 to 6
- norm_gain: float32 [1024], replicated, may hold values from 0.1 to 1.9
- w_query: bfloat16 [1024, 1024], P(None, 'head'), may hold values from -5.0375 to 5.0375
- w_key: bfloat16 [1024, 1024], P(None, 'head'), may hold values from -5.0375 to 5.0375
- w_value: bfloat16 [1024, 1024], P(None, 'head'), may hold values from -0.1875 to 0.1875
- w_out: bfloat16 [1024, 1024], P('head'), may hold values from -0.25 to 0.25
- cluster_ids: int32 [16, 6144, 1], P('head', ('docs', 'seq')), parts along dimension 1, may hold values from 0 to 255; in each aligned block of 768 rows (0 to 767, 768 to 1535, ..., all dimensions but the last counted through in order) at most 6 rows name the same one
Outputs:
- layer_out: bfloat16 [6144, 1024], P(('docs', 'seq'), 'head'), parts along dimension 0
The draws below stay inside these ranges and needn't reach their ends.
There are 2 independent parts, one for each index of `docs`. The reference program is written for one: setup_inputs(seed, part) draws one part's arguments, and reference() takes and returns one part's arrays. A program takes and returns all parts, laid end to end along the dimension named above; an argument that names none is the same for every part. Nothing has to cross between parts.
Inputs may be any that keep to these rules, and one draw needn't show every extreme that they name: `cluster_ids`: among the 768 tokens of one index of seq, at most 6 name the same cluster in one head, a bound that some block reaches so.
All inputs are finite; a program needn't handle non-finite values.
Results may differ from the reference program's by a relative error of at most 0.0055.
Values may be sent and summed in bfloat16 or wider, within the bound.
A program may use at most 64 MiB of HBM per device.

```python
import math
import jax
import jax.numpy as jnp
import numpy as np
from jax import lax

D = 1024
HEADS = 16
HEAD_DIM = 64
CLUSTERS = 256
TOK_DEV = 768
CAPACITY = 6
TOKENS = 3072
N_SEQ = 4


def shared_base(key):
    return jnp.clip(jax.random.normal(key, (D, HEADS * HEAD_DIM), jnp.float32), -4.0, 4.0)


def draw_w_query(key, part):
    base = shared_base(key)
    return (base * D ** (-0.5)).astype(jnp.bfloat16)


def draw_w_key(key, part):
    key = jax.random.fold_in(key, 5)
    own = jnp.clip(jax.random.normal(jax.random.fold_in(key, 1), (D, HEADS * HEAD_DIM), jnp.float32), -4.0, 4.0)
    return (own * D ** (-0.5)).astype(jnp.bfloat16)


def with_spikes(values, rng, source, target, shards_of, factor):
    def block_of(dim):
        return (jnp.arange(values.shape[dim]) // (values.shape[dim] // shards_of)).reshape((-1,) + (1,) * (values.ndim - 1 - dim))

    one_side = jax.random.permutation(rng, shards_of)[block_of(target)]
    other_side = (block_of(target) + shards_of // 2) % shards_of
    return jnp.where((block_of(source) == one_side) | (block_of(source) == other_side), factor * values, values)


def level_of(rng, dims, cuts, low, largest):
    factor_of = 1.0
    for position, parts in cuts:
        draws = jax.random.uniform(jax.random.fold_in(jax.random.fold_in(rng, 6), position), (parts,), jnp.float32, low / len(cuts), largest / len(cuts))
        factor_of = factor_of * jnp.repeat(jnp.exp(draws), dims[position] // parts).reshape((-1,) + (1,) * (len(dims) - 1 - position))
    return factor_of


def deal_out(own_key, own, number, rows, count, top, most, slope):
    order = jax.random.permutation(own_key, count)
    packed, usual = portions_of(count, rows * top, most, slope, True), portions_of(count, rows * top, most, slope, False)
    places = jnp.arange(count)

    def named(sizes, turn):
        used = int((sizes > 0).sum())
        fixed = max(1, used // 4)
        moved = fixed + (places - fixed + turn * (used - fixed)) % max(1, count - fixed)
        return jnp.zeros((count,), jnp.int32).at[order[jnp.where(places < fixed, places, moved)]].set(jnp.asarray(sizes, jnp.int32))

    sizes = jnp.where(number % 4 == 0, named(packed, number // 4), named(usual, number - number // 4 - 1))
    mixed = jax.random.permutation(jax.random.fold_in(own, 3), count)
    donor, sink = mixed[0:count // 2 * 2:2], mixed[1:count // 2 * 2:2]
    slack = jnp.minimum(sizes[donor] - 1, most - sizes[sink]) // 2
    slack = jnp.where((donor == order[0]) | (sink == order[0]) | (sizes[sink] == 0), 0, jnp.maximum(slack, 0))
    moved = jax.random.randint(jax.random.fold_in(own, 4), (count // 2,), 0, 1 << 20) % (slack + 1)
    sizes = sizes.at[donor].add(-moved).at[sink].add(moved)
    labels = jnp.searchsorted(jnp.cumsum(sizes), jnp.arange(rows * top), side="right").astype(jnp.int32)
    grid = labels.reshape(top, rows).T
    grid = grid[jax.random.permutation(jax.random.fold_in(own, 1), rows)]
    turn = jax.random.randint(jax.random.fold_in(own, 2), (rows, 1), 0, top)
    return jnp.take_along_axis(grid, (jnp.arange(top)[None, :] + turn) % top, axis=1)


def portions_of(amount, total, most, slope, full):
    loads = [(1 << 20) // math.isqrt(rank ** slope) + 1 for rank in range(1, amount + 1)]
    largest = most if full else min(most, max(-(-total // amount), total * loads[0] // sum(loads)))
    least = 1 if total - largest >= amount - 1 else 0
    counts, rest = [largest] + [least] * (amount - 1), total - largest - least * (amount - 1)
    while rest > 0:
        movable = [i for i in range(1, amount) if counts[i] < largest] or [i for i in range(1, amount) if counts[i] < most]
        pool, left = sum([loads[i] for i in movable]), rest
        for i in movable:
            more = min(most - counts[i], max(1, left * loads[i] // pool), rest)
            counts[i] = counts[i] + more
            rest = rest - more
    return np.array(counts)


def scatter_about(rng, extent, spread, limit, pieces=(), kind=jnp.bfloat16):
    entries = spread * jax.random.normal(rng, extent, jnp.float32)
    if pieces:
        entries = entries * level_of(rng, extent, pieces, -0.22, 0.18)
    return jnp.clip(entries, -limit, limit).astype(kind)


def heavy_noise(rng, dims, width, limit, cuts, heavy, held_as=jnp.bfloat16):
    entries = width * jax.random.normal(rng, dims, jnp.float32)
    if cuts:
        entries = entries * level_of(rng, dims, cuts, -0.22, 0.18)
    return jnp.clip(with_spikes(entries, jax.random.fold_in(rng, 3), *heavy), -limit, limit).astype(held_as)


def setup_inputs(seed: int = 0, part: int = 0) -> dict:
    streams_of = jax.random.split(jax.random.key(seed), 8)
    part_keys = jax.random.split(jax.random.fold_in(streams_of[7], part), 8)
    tokens = scatter_about(part_keys[0], (TOKENS, D), 1.0, 6.0, ((0, 4), (1, 4)))
    norm_gain = jnp.clip(1.0 + 0.18 * jax.random.normal(streams_of[1], (D,), jnp.float32), 0.1, 1.9)
    w_query = draw_w_query(jax.random.fold_in(streams_of[7], 71), part)
    w_key = draw_w_key(jax.random.fold_in(streams_of[7], 71), part)
    w_value = scatter_about(streams_of[4], (D, HEADS * HEAD_DIM), D ** -0.5, 0.1875, ((1, 4),))
    w_out = heavy_noise(streams_of[5], (HEADS * HEAD_DIM, D), (HEADS * HEAD_DIM) ** -0.5, 0.25, ((0, 4),), (0, 1, 4, 2.0))
    cluster_ids_keys = jax.random.split(jax.random.fold_in(part_keys[6], 1), HEADS * TOKENS // TOK_DEV)
    cluster_ids_turns = jax.random.permutation(jax.random.fold_in(part_keys[6], 3), HEADS * TOKENS // TOK_DEV)
    cluster_ids = jax.vmap(lambda own, number: deal_out(jax.random.fold_in(part_keys[6], 2), own, number, TOK_DEV, CLUSTERS, 1, CAPACITY, 2))(cluster_ids_keys, cluster_ids_turns).reshape((HEADS, TOKENS, 1))
    return dict(tokens=tokens, norm_gain=norm_gain, w_query=w_query, w_key=w_key, w_value=w_value, w_out=w_out, cluster_ids=cluster_ids)


def cluster_attention(cq, ck, cv, live):
    scores = jnp.einsum('csd,ctd->cst', cq.astype(jnp.float32), ck.astype(jnp.float32)) * HEAD_DIM ** (-0.5)
    scores = jnp.where(live[:, None, :], scores, jnp.float32(-1e+30))
    top = lax.optimization_barrier(jnp.max(scores, axis=-1, keepdims=True))
    expo = jnp.exp(scores - top)
    weights = (expo / lax.optimization_barrier(jnp.sum(expo, axis=-1, keepdims=True))).astype(jnp.bfloat16)
    return jnp.einsum('cst,ctd->csd', weights.astype(jnp.float32), cv.astype(jnp.float32)).astype(jnp.bfloat16)

def one_head(operands):
    head_q, head_k, head_v, head_ids = operands
    slots = N_SEQ * CAPACITY
    order = jnp.argsort(head_ids, stable=True).astype(jnp.int32)
    sorted_ids = head_ids[order].astype(jnp.int32)
    starts = jnp.searchsorted(sorted_ids, jnp.arange(CLUSTERS, dtype=jnp.int32)).astype(jnp.int32)
    rank = jnp.arange(TOKENS, dtype=jnp.int32) - starts[sorted_ids]
    table = jnp.full((CLUSTERS, slots), TOKENS, jnp.int32).at[sorted_ids, rank].set(order)
    live = table < TOKENS
    filler = jnp.zeros((1, HEAD_DIM), jnp.bfloat16)
    cq = jnp.concatenate([head_q, filler], axis=0)[table]
    ck = jnp.concatenate([head_k, filler], axis=0)[table]
    cv = jnp.concatenate([head_v, filler], axis=0)[table]
    result = cluster_attention(cq, ck, cv, live)
    placed = jnp.zeros((TOKENS + 1, HEAD_DIM), jnp.bfloat16).at[table.reshape(-1)].set(result.reshape(-1, HEAD_DIM))
    return placed[:TOKENS]

def reference(tokens, norm_gain, w_query, w_key, w_value, w_out, cluster_ids):
    inputs = tokens.astype(jnp.float32)
    square = lax.optimization_barrier(jnp.mean(inputs * inputs, axis=-1, keepdims=True))
    normed = (inputs * lax.rsqrt(square + 1e-05) * norm_gain).astype(jnp.bfloat16)

    def project(weight):
        full = jnp.dot(normed, weight, preferred_element_type=jnp.float32).astype(jnp.bfloat16)
        return full.reshape(TOKENS, HEADS, HEAD_DIM).transpose(1, 0, 2)
    queries = project(w_query)
    keys = project(w_key)
    values = project(w_value)
    attended = lax.map(one_head, (queries, keys, values, cluster_ids[:, :, 0]))
    attended = attended.transpose(1, 0, 2).reshape(TOKENS, HEADS * HEAD_DIM)
    branch = jnp.dot(attended, w_out, preferred_element_type=jnp.float32)
    return (inputs + branch).astype(jnp.bfloat16)
```

```python
import functools

import jax
import jax.numpy as jnp
from jax import lax
from jax.experimental import pallas as pl
from jax.experimental.pallas import tpu as pltpu
from jax.sharding import PartitionSpec as P

HEAD_DIM = 64
CLUSTERS = 256
CAPACITY = 6


def attend_block(received, marks, n_seq):
    count = received.shape[1]
    span = n_seq * CAPACITY
    parts = received.reshape(3, count, span, HEAD_DIM)
    live = marks.reshape(count, span) > 0.5
    scores = jnp.einsum(
        "csd,ctd->cst", parts[0], parts[1], preferred_element_type=jnp.float32
    ) * HEAD_DIM ** (-0.5)
    scores = jnp.where(live[:, None, :], scores, jnp.float32(-1e30))
    top = jnp.max(scores, axis=-1, keepdims=True)
    expo = jnp.exp(scores - top)
    weights = (expo / jnp.sum(expo, axis=-1, keepdims=True)).astype(jnp.bfloat16)
    result = jnp.einsum(
        "cst,ctd->csd", weights, parts[2], preferred_element_type=jnp.float32
    ).astype(jnp.bfloat16)
    return result.reshape(count, n_seq, CAPACITY * HEAD_DIM)


def place_head(operands):
    head_slot, head_parts = operands
    columns = jnp.arange(CLUSTERS * CAPACITY, dtype=jnp.int32)
    onehot = (head_slot[:, None] == columns[None, :]).astype(jnp.bfloat16)
    placed = jnp.einsum(
        "ts,ctd->csd", onehot, head_parts, preferred_element_type=jnp.float32
    ).astype(jnp.bfloat16)
    filled = jnp.sum(onehot, axis=0, dtype=jnp.float32).astype(jnp.bfloat16)
    return (placed, filled)


def fetch_head(operands):
    head_slot, head_back = operands
    columns = jnp.arange(CLUSTERS * CAPACITY, dtype=jnp.int32)
    onehot = (head_slot[:, None] == columns[None, :]).astype(jnp.bfloat16)
    return jnp.dot(onehot, head_back, preferred_element_type=jnp.float32).astype(jnp.bfloat16)


def clustered(tokens, norm_gain, w_query, w_key, w_value, w_out, cluster_ids):
    n_seq = lax.axis_size("seq")
    tok = tokens.shape[0]
    heads_here = w_query.shape[1] // HEAD_DIM
    owned = CLUSTERS // n_seq
    rows = lax.all_gather(tokens, "head", axis=1, tiled=True)
    inputs = rows.astype(jnp.float32)
    square = jnp.mean(inputs * inputs, axis=-1, keepdims=True)
    normed = (inputs * lax.rsqrt(square + 1e-05) * norm_gain).astype(jnp.bfloat16)
    queries = jnp.dot(normed, w_query, preferred_element_type=jnp.float32).astype(jnp.bfloat16)
    keys = jnp.dot(normed, w_key, preferred_element_type=jnp.float32).astype(jnp.bfloat16)
    values = jnp.dot(normed, w_value, preferred_element_type=jnp.float32).astype(jnp.bfloat16)
    ids = cluster_ids[:, :, 0]
    owner = ids // owned
    within = ids % owned
    positions = jnp.arange(tok, dtype=jnp.int32)
    earlier = positions[None, :] < positions[:, None]
    same = (ids[:, :, None] == ids[:, None, :]) & earlier[None, :, :]
    rank = jnp.sum(same.astype(jnp.int32), axis=2)
    slot_local = (within * n_seq + owner) * CAPACITY + rank
    stacked = jnp.stack([queries, keys, values]).reshape(3, tok, heads_here, HEAD_DIM)
    stacked = stacked.transpose(2, 0, 1, 3)
    placed, filled = lax.map(place_head, (slot_local, stacked))
    outgoing = placed.transpose(1, 0, 2, 3).reshape(
        3, heads_here * owned, n_seq, CAPACITY * HEAD_DIM
    )
    out_marks = filled.reshape(1, heads_here * owned, n_seq, CAPACITY)
    received, in_marks = (
        lax.all_to_all(outgoing, "seq", split_axis=2, concat_axis=2, tiled=True),
        lax.all_to_all(out_marks, "seq", split_axis=2, concat_axis=2, tiled=True),
    )
    result = attend_block(received, in_marks, n_seq)
    returned = lax.all_to_all(result, "seq", split_axis=1, concat_axis=1, tiled=True)
    back_heads = returned.reshape(heads_here, CLUSTERS * CAPACITY, HEAD_DIM)
    fetched = lax.map(fetch_head, (slot_local, back_heads))
    attended = fetched.transpose(1, 0, 2).reshape(tok, heads_here * HEAD_DIM)
    partial_sums = jnp.dot(attended, w_out, preferred_element_type=jnp.float32)
    share = lax.psum_scatter(partial_sums, "head", scatter_dimension=1, tiled=True)
    return (tokens.astype(jnp.float32) + share).astype(jnp.bfloat16)


CHUNK = 256
HALF = CHUNK // 2
MESH = pl.DeviceIdType.MESH
LOG2E = 1.4426950408889634


def remote(src, dst, send, recv, where):
    return pltpu.make_async_remote_copy(
        src_ref=src, dst_ref=dst, send_sem=send, recv_sem=recv, device_id=where, device_id_type=MESH
    )


def layer_kernel(
    n_seq, n_head, tok_ref, gain_ref, wq_ref, wk_ref, wv_ref, wo_ref, ids_ref, out_ref,
    xfull, kv_out, kv_in, q_out, q_in, id_in, ret, back, wo_in, w_top, w_bot, sbuf,
    tok_send, tok_recv, wo_send, wo_recv, id_send, id_recv, kv_send, kv_recv,
    q_send, q_recv, ret_send, ret_recv, rl_send, rl_recv,
):
    s = lax.axis_index("seq")
    h = lax.axis_index("head")
    tok, width = tok_ref.shape
    chunks = tok // CHUNK
    sib = h + 1 - 2 * lax.rem(h, 2)
    par = lax.rem(h + 2, 4)
    dia = lax.rem(sib + 2, 4)
    seq_at = [lax.rem(s + i, n_seq) for i in range(n_seq)]
    seq_from = [lax.rem(s + n_seq - i, n_seq) for i in range(n_seq)]
    head_at = [lax.rem(h + j, n_head) for j in range(n_head)]
    head_from = [lax.rem(h + n_head - j, n_head) for j in range(n_head)]

    barrier = pltpu.get_barrier_semaphore()
    for i in range(1, n_seq):
        pl.semaphore_signal(barrier, inc=1, device_id={"seq": seq_at[i]}, device_id_type=MESH)
    for j in range(1, n_head):
        pl.semaphore_signal(barrier, inc=1, device_id={"head": head_at[j]}, device_id_type=MESH)
    pl.semaphore_wait(barrier, n_seq + n_head - 2)

    def rows(c):
        return pl.ds(pl.multiple_of(c * CHUNK, CHUNK), CHUNK)

    def packed(c):
        return pl.ds(pl.multiple_of(c * HALF, HALF), HALF)

    started = []

    def tok_copy(kind, c, owner, to):
        src = tok_ref.at[rows(c)] if kind < 2 else xfull.at[owner, rows(c)]
        return remote(src, xfull.at[owner, rows(c)], tok_send.at[kind, c], tok_recv.at[kind, c], {"head": to})

    for c in range(chunks):
        for kind, to in ((0, par), (1, sib)):
            copy = tok_copy(kind, c, h, to)
            copy.start()
            started.append(copy)
    for i in range(1, n_seq):
        copy = remote(ids_ref.at[seq_at[i]], id_in.at[s], id_send.at[i], id_recv.at[i], {"seq": seq_at[i]})
        copy.start()
        started.append(copy)
    for j in range(1, n_head):
        cols = pl.ds(pl.multiple_of(head_at[j] * width, width), width)
        copy = remote(wo_ref.at[:, cols], wo_in.at[h], wo_send.at[j], wo_recv.at[j], {"head": head_at[j]})
        copy.start()
        started.append(copy)
    xfull[h] = tok_ref[...]
    id_in[s] = ids_ref[s]
    wo_in[h] = wo_ref[:, pl.ds(pl.multiple_of(h * width, width), width)]
    w_top[...] = jnp.zeros_like(w_top)
    w_bot[...] = jnp.zeros_like(w_bot)

    lane = lax.broadcasted_iota(jnp.int32, (HALF, 2 * HEAD_DIM), 1)
    low = lane < HEAD_DIM

    for c in range(chunks):
        tok_copy(0, c, par, par).wait_recv()
        copy = tok_copy(2, c, par, sib)
        copy.start()
        started.append(copy)
        tok_copy(1, c, sib, sib).wait_recv()
        tok_copy(2, c, dia, sib).wait_recv()
        here = pl.ds(c * CHUNK, CHUNK)
        x = jnp.concatenate([xfull[g, here].astype(jnp.float32) for g in range(n_head)], axis=1)
        square = jnp.sum(x * x, axis=1, keepdims=True) * (1.0 / x.shape[1])
        normed = (x * lax.rsqrt(square + 1e-05) * gain_ref[...]).astype(jnp.bfloat16)
        k = jnp.dot(normed, wk_ref[...], preferred_element_type=jnp.float32)
        v = jnp.dot(normed, wv_ref[...], preferred_element_type=jnp.float32)
        for t in range(n_seq):
            cols = slice(t * HEAD_DIM, (t + 1) * HEAD_DIM)
            kv_out[t, here] = jnp.concatenate([k[:, cols], v[:, cols]], axis=1).astype(jnp.bfloat16)
        for i in range(1, n_seq):
            copy = remote(
                kv_out.at[seq_at[i], here], kv_in.at[s, here],
                kv_send.at[i, c], kv_recv.at[i, c], {"seq": seq_at[i]},
            )
            copy.start()
            started.append(copy)
        kv_in[s, here] = kv_out[s, here]
        q = jnp.dot(normed, wq_ref[...], preferred_element_type=jnp.float32)
        pack = pl.ds(c * HALF, HALF)
        for t in range(n_seq):
            cols = slice(t * HEAD_DIM, (t + 1) * HEAD_DIM)
            q_out[t, pack] = jnp.concatenate([q[:HALF, cols], q[HALF:, cols]], axis=1).astype(jnp.bfloat16)
    for c in range(chunks):
        pack = pl.ds(c * HALF, HALF)
        for i in range(1, n_seq):
            copy = remote(
                q_out.at[seq_at[i], pack], q_in.at[s, pack],
                q_send.at[i, c], q_recv.at[i, c], {"seq": seq_at[i]},
            )
            copy.start()
            started.append(copy)
    q_in[s] = q_out[s]

    for j in range(1, n_head):
        remote(
            wo_ref.at[:, pl.ds(0, width)], wo_in.at[head_from[j]], wo_send.at[j], wo_recv.at[j],
            {"head": head_from[j]},
        ).wait_recv()
    for g in range(n_head):
        for t in range(n_seq):
            part = wo_in[g, t * HEAD_DIM:(t + 1) * HEAD_DIM, :]
            at = (g * n_seq + t) * 2 * HEAD_DIM
            w_top[at:at + HEAD_DIM, :] = part
            w_bot[at + HEAD_DIM:at + 2 * HEAD_DIM, :] = part
    for i in range(1, n_seq):
        remote(
            ids_ref.at[seq_from[i]], id_in.at[seq_from[i]], id_send.at[i], id_recv.at[i],
            {"seq": seq_from[i]},
        ).wait_recv()
    for c in range(chunks):
        for i in range(1, n_seq):
            here = pl.ds(c * CHUNK, CHUNK)
            remote(
                kv_out.at[seq_from[i], here], kv_in.at[seq_from[i], here],
                kv_send.at[i, c], kv_recv.at[i, c], {"seq": seq_from[i]},
            ).wait_recv()

    def attend(source, c):
        pair = q_in[source, packed(c)].astype(jnp.float32)
        turned = pltpu.roll(pair, HEAD_DIM, 1)
        query = jnp.concatenate(
            [jnp.where(low, pair, 0.0), jnp.where(low, turned, 0.0)], axis=0
        ).astype(jnp.bfloat16)
        own = jnp.broadcast_to(id_in[source, c, 0:1, :], (CHUNK, CHUNK)).T
        top = None
        for block in range(n_seq * chunks):
            j, e = block // chunks, block % chunks
            kv = kv_in[j, e * CHUNK:(e + 1) * CHUNK, :]
            score = lax.dot_general(query, kv, (((1,), (1,)), ((), ())), preferred_element_type=jnp.float32)
            score = jnp.where(own == id_in[j, e, 0:1, :], score, jnp.float32(-1e30))
            sbuf[:, block * CHUNK:(block + 1) * CHUNK] = score
            peak = jnp.maximum(score[:, :HALF], score[:, HALF:])
            top = peak if top is None else jnp.maximum(top, peak)
        top = jnp.max(top, axis=1, keepdims=True)
        total = None
        acc = None
        for block in range(n_seq * chunks):
            j, e = block // chunks, block % chunks
            kv = kv_in[j, e * CHUNK:(e + 1) * CHUNK, :]
            score = sbuf[:, block * CHUNK:(block + 1) * CHUNK]
            expo = jnp.exp2((score - top) * jnp.float32(LOG2E * HEAD_DIM ** -0.5))
            summed = expo[:, :HALF] + expo[:, HALF:]
            total = summed if total is None else total + summed
            term = jnp.dot(expo.astype(jnp.bfloat16), kv, preferred_element_type=jnp.float32)
            acc = term if acc is None else acc + term
        result = acc / jnp.sum(total, axis=1, keepdims=True)
        return jnp.where(low, pltpu.roll(result[:HALF], HEAD_DIM, 1), result[HALF:]).astype(jnp.bfloat16)

    def ret_copy(i, c, slot, to):
        return remote(
            ret.at[i, packed(c)], back.at[h, slot, packed(c)],
            ret_send.at[i, c], ret_recv.at[i, c], {"seq": to},
        )

    def relay(i, c, j, owner, to):
        slot = lax.rem(s + n_seq - i, n_seq)
        return remote(
            back.at[owner, slot, packed(c)], back.at[owner, slot, packed(c)],
            rl_send.at[j, i, c], rl_recv.at[j, i, c], {"head": to},
        )

    def pass_on(i, c):
        for j in range(1, n_head):
            relay(i, c, j, h, head_at[j]).start()

    def back_wait(i, c):
        sender = lax.rem(s + n_seq - i, n_seq)
        ret_copy(i, c, sender, sender).wait_recv()

    @pl.loop(0, n_seq)
    def _(i):
        source = lax.rem(s + i, n_seq)

        @pl.loop(0, chunks)
        def _(c):
            @pl.when(i > 0)
            def _():
                remote(
                    q_out.at[source, packed(c)], q_in.at[source, packed(c)],
                    q_send.at[n_seq - i, c], q_recv.at[n_seq - i, c], {"seq": source},
                ).wait_recv()

            result = attend(source, c)

            @pl.when(i == 0)
            def _():
                back[h, s, packed(c)] = result
                pass_on(0, c)

            @pl.when(i > 0)
            def _():
                ret[i, packed(c)] = result
                ret_copy(i, c, s, source).start()

            @pl.when(i > 1)
            def _():
                back_wait(i - 1, c)
                pass_on(i - 1, c)

    for c in range(chunks):
        back_wait(n_seq - 1, c)
        pass_on(n_seq - 1, c)
    for c in range(chunks):
        for i in range(n_seq):
            for j in range(1, n_head):
                relay(i, c, j, head_from[j], head_from[j]).wait_recv()
        pack = pl.ds(c * HALF, HALF)
        mixed = jnp.concatenate([back[g, t, pack] for g in range(n_head) for t in range(n_seq)], axis=1)
        for weight, at in ((w_top, c * CHUNK), (w_bot, c * CHUNK + HALF)):
            branch = jnp.dot(mixed, weight[...], preferred_element_type=jnp.float32)
            out_ref[at:at + HALF, :] = (tok_ref[at:at + HALF, :].astype(jnp.float32) + branch).astype(jnp.bfloat16)
    for copy in started:
        copy.wait_send()
    for c in range(chunks):
        for i in range(n_seq):
            if i > 0:
                ret_copy(i, c, s, seq_at[i]).wait_send()
            for j in range(1, n_head):
                relay(i, c, j, h, head_at[j]).wait_send()


def dense(tokens, norm_gain, w_query, w_key, w_value, w_out, cluster_ids):
    n_seq, n_head = lax.axis_size("seq"), lax.axis_size("head")
    tok, width = tokens.shape
    chunks = tok // CHUNK
    ids = cluster_ids[:, :, 0].astype(jnp.float32).reshape(n_seq, chunks, 1, CHUNK)
    ids = jnp.broadcast_to(ids, (n_seq, chunks, 8, CHUNK))
    pair = 2 * HEAD_DIM
    bf16, f32 = jnp.bfloat16, jnp.float32
    vmem, dma = pltpu.VMEM, pltpu.SemaphoreType.DMA
    return pl.pallas_call(
        functools.partial(layer_kernel, n_seq, n_head),
        out_shape=jax.ShapeDtypeStruct((tok, width), bf16),
        in_specs=[pl.BlockSpec(memory_space=pltpu.VMEM)] * 7,
        out_specs=pl.BlockSpec(memory_space=pltpu.VMEM),
        scratch_shapes=[
            vmem((n_head, tok, width), bf16),
            vmem((n_seq, tok, pair), bf16),
            vmem((n_seq, tok, pair), bf16),
            vmem((n_seq, tok // 2, pair), bf16),
            vmem((n_seq, tok // 2, pair), bf16),
            vmem((n_seq, chunks, 8, CHUNK), f32),
            vmem((n_seq, tok // 2, pair), bf16),
            vmem((n_head, n_seq, tok // 2, pair), bf16),
            vmem((n_head, width, width), bf16),
            vmem((n_head * n_seq * pair, width), bf16),
            vmem((n_head * n_seq * pair, width), bf16),
            vmem((CHUNK, n_seq * tok), f32),
            dma((3, chunks)), dma((3, chunks)),
            dma((n_head,)), dma((n_head,)),
            dma((n_seq,)), dma((n_seq,)),
            dma((n_seq, chunks)), dma((n_seq, chunks)),
            dma((n_seq, chunks)), dma((n_seq, chunks)),
            dma((n_seq, chunks)), dma((n_seq, chunks)),
            dma((n_head, n_seq, chunks)), dma((n_head, n_seq, chunks)),
        ],
        compiler_params=pltpu.CompilerParams(
            collective_id=0, has_side_effects=True, vmem_limit_bytes=48 * 1024 * 1024
        ),
    )(tokens, norm_gain.reshape(1, -1), w_query, w_key, w_value, w_out, ids)


def on_device(*operands):
    tokens, w_query = operands[0], operands[2]
    n_seq, n_head = lax.axis_size("seq"), lax.axis_size("head")
    heads_here = w_query.shape[1] // HEAD_DIM
    if n_head == 4 and heads_here == n_seq and tokens.shape[0] % CHUNK == 0 and n_seq > 1:
        return dense(*operands)
    return clustered(*operands)


def solution(mesh):
    return jax.shard_map(
        on_device,
        mesh=mesh,
        in_specs=(
            P(("docs", "seq"), "head"),
            P(),
            P(None, "head"),
            P(None, "head"),
            P(None, "head"),
            P("head", None),
            P("head", ("docs", "seq"), None),
        ),
        out_specs=P(("docs", "seq"), "head"),
        check_vma=False,
    )
```

```python
import functools

import jax
import jax.numpy as jnp
from jax import lax
from jax.experimental import pallas as pl
from jax.experimental.pallas import tpu as pltpu
from jax.sharding import PartitionSpec as P

HEAD_DIM = 64
CLUSTERS = 256
CAPACITY = 6


def attend_block(received, marks, n_seq):
    count = received.shape[1]
    span = n_seq * CAPACITY
    parts = received.reshape(3, count, span, HEAD_DIM)
    live = marks.reshape(count, span) > 0.5
    scores = jnp.einsum(
        "csd,ctd->cst", parts[0], parts[1], preferred_element_type=jnp.float32
    ) * HEAD_DIM ** (-0.5)
    scores = jnp.where(live[:, None, :], scores, jnp.float32(-1e30))
    top = jnp.max(scores, axis=-1, keepdims=True)
    expo = jnp.exp(scores - top)
    weights = (expo / jnp.sum(expo, axis=-1, keepdims=True)).astype(jnp.bfloat16)
    result = jnp.einsum(
        "cst,ctd->csd", weights, parts[2], preferred_element_type=jnp.float32
    ).astype(jnp.bfloat16)
    return result.reshape(count, n_seq, CAPACITY * HEAD_DIM)


def place_head(operands):
    head_slot, head_parts = operands
    columns = jnp.arange(CLUSTERS * CAPACITY, dtype=jnp.int32)
    onehot = (head_slot[:, None] == columns[None, :]).astype(jnp.bfloat16)
    placed = jnp.einsum(
        "ts,ctd->csd", onehot, head_parts, preferred_element_type=jnp.float32
    ).astype(jnp.bfloat16)
    filled = jnp.sum(onehot, axis=0, dtype=jnp.float32).astype(jnp.bfloat16)
    return (placed, filled)


def fetch_head(operands):
    head_slot, head_back = operands
    columns = jnp.arange(CLUSTERS * CAPACITY, dtype=jnp.int32)
    onehot = (head_slot[:, None] == columns[None, :]).astype(jnp.bfloat16)
    return jnp.dot(onehot, head_back, preferred_element_type=jnp.float32).astype(jnp.bfloat16)


def clustered(tokens, norm_gain, w_query, w_key, w_value, w_out, cluster_ids):
    n_seq = lax.axis_size("seq")
    tok = tokens.shape[0]
    heads_here = w_query.shape[1] // HEAD_DIM
    owned = CLUSTERS // n_seq
    rows = lax.all_gather(tokens, "head", axis=1, tiled=True)
    inputs = rows.astype(jnp.float32)
    square = jnp.mean(inputs * inputs, axis=-1, keepdims=True)
    normed = (inputs * lax.rsqrt(square + 1e-05) * norm_gain).astype(jnp.bfloat16)
    queries = jnp.dot(normed, w_query, preferred_element_type=jnp.float32).astype(jnp.bfloat16)
    keys = jnp.dot(normed, w_key, preferred_element_type=jnp.float32).astype(jnp.bfloat16)
    values = jnp.dot(normed, w_value, preferred_element_type=jnp.float32).astype(jnp.bfloat16)
    ids = cluster_ids[:, :, 0]
    owner = ids // owned
    within = ids % owned
    positions = jnp.arange(tok, dtype=jnp.int32)
    earlier = positions[None, :] < positions[:, None]
    same = (ids[:, :, None] == ids[:, None, :]) & earlier[None, :, :]
    rank = jnp.sum(same.astype(jnp.int32), axis=2)
    slot_local = (within * n_seq + owner) * CAPACITY + rank
    stacked = jnp.stack([queries, keys, values]).reshape(3, tok, heads_here, HEAD_DIM)
    stacked = stacked.transpose(2, 0, 1, 3)
    placed, filled = lax.map(place_head, (slot_local, stacked))
    outgoing = placed.transpose(1, 0, 2, 3).reshape(
        3, heads_here * owned, n_seq, CAPACITY * HEAD_DIM
    )
    out_marks = filled.reshape(1, heads_here * owned, n_seq, CAPACITY)
    received, in_marks = (
        lax.all_to_all(outgoing, "seq", split_axis=2, concat_axis=2, tiled=True),
        lax.all_to_all(out_marks, "seq", split_axis=2, concat_axis=2, tiled=True),
    )
    result = attend_block(received, in_marks, n_seq)
    returned = lax.all_to_all(result, "seq", split_axis=1, concat_axis=1, tiled=True)
    back_heads = returned.reshape(heads_here, CLUSTERS * CAPACITY, HEAD_DIM)
    fetched = lax.map(fetch_head, (slot_local, back_heads))
    attended = fetched.transpose(1, 0, 2).reshape(tok, heads_here * HEAD_DIM)
    partial_sums = jnp.dot(attended, w_out, preferred_element_type=jnp.float32)
    share = lax.psum_scatter(partial_sums, "head", scatter_dimension=1, tiled=True)
    return (tokens.astype(jnp.float32) + share).astype(jnp.bfloat16)


CHUNK = 256
HALF = CHUNK // 2
MESH = pl.DeviceIdType.MESH
LOG2E = 1.4426950408889634


def remote(src, dst, send, recv, where):
    return pltpu.make_async_remote_copy(
        src_ref=src, dst_ref=dst, send_sem=send, recv_sem=recv, device_id=where, device_id_type=MESH
    )


def layer_kernel(
    n_seq, n_head, tok_ref, gain_hbm, wq_hbm, wk_hbm, wv_hbm, wo_ref, ids_ref, out_ref,
    gain_ref, wq_ref, wk_ref, wv_ref, load_sem,
    xfull, kv_out, kv_in, q_out, q_in, id_in, ret, back, wo_in, w_top, w_bot, sbuf,
    tok_send, tok_recv, wo_send, wo_recv, id_send, id_recv, kv_send, kv_recv,
    q_send, q_recv, ret_send, ret_recv, rl_send, rl_recv,
):
    s = lax.axis_index("seq")
    h = lax.axis_index("head")
    tok, width = tok_ref.shape
    chunks = tok // CHUNK
    sib = h + 1 - 2 * lax.rem(h, 2)
    par = lax.rem(h + 2, 4)
    dia = lax.rem(sib + 2, 4)
    seq_at = [lax.rem(s + i, n_seq) for i in range(n_seq)]
    seq_from = [lax.rem(s + n_seq - i, n_seq) for i in range(n_seq)]
    head_at = [lax.rem(h + j, n_head) for j in range(n_head)]
    head_from = [lax.rem(h + n_head - j, n_head) for j in range(n_head)]

    own_cols = pl.ds(pl.multiple_of(h * width, width), width)
    loads = [
        pltpu.make_async_copy(src, dst, load_sem.at[n])
        for n, (src, dst) in enumerate((
            (tok_ref, xfull.at[h]), (gain_hbm, gain_ref), (wk_hbm, wk_ref), (wv_hbm, wv_ref), (wq_hbm, wq_ref),
            (wo_ref.at[:, own_cols], wo_in.at[h]), (ids_ref.at[s], id_in.at[s]),
        ))
    ]
    for load in loads:
        load.start()
    barrier = pltpu.get_barrier_semaphore()
    for i in range(1, n_seq):
        pl.semaphore_signal(barrier, inc=1, device_id={"seq": seq_at[i]}, device_id_type=MESH)
    for j in range(1, n_head):
        pl.semaphore_signal(barrier, inc=1, device_id={"head": head_at[j]}, device_id_type=MESH)
    pl.semaphore_wait(barrier, n_seq + n_head - 2)

    def rows(c):
        return pl.ds(pl.multiple_of(c * CHUNK, CHUNK), CHUNK)

    def packed(c):
        return pl.ds(pl.multiple_of(c * HALF, HALF), HALF)

    started = []

    def tok_copy(kind, c, owner, to):
        src = tok_ref.at[rows(c)] if kind < 2 else xfull.at[owner, rows(c)]
        return remote(src, xfull.at[owner, rows(c)], tok_send.at[kind, c], tok_recv.at[kind, c], {"head": to})

    for c in range(chunks):
        for kind, to in ((0, par), (1, sib)):
            copy = tok_copy(kind, c, h, to)
            copy.start()
            started.append(copy)
    for i in range(1, n_seq):
        copy = remote(ids_ref.at[seq_at[i]], id_in.at[s], id_send.at[i], id_recv.at[i], {"seq": seq_at[i]})
        copy.start()
        started.append(copy)
    w_top[...] = jnp.zeros_like(w_top)
    w_bot[...] = jnp.zeros_like(w_bot)

    def query_copy(i, c):
        return remote(
            q_out.at[lax.rem(s + i, n_seq), packed(c)], q_in.at[s, packed(c)],
            q_send.at[i, c], q_recv.at[i, c], {"seq": lax.rem(s + i, n_seq)},
        )

    def send_queries(i):
        for c in range(chunks):
            query_copy(i, c).start()

    lane = lax.broadcasted_iota(jnp.int32, (HALF, 2 * HEAD_DIM), 1)
    low = lane < HEAD_DIM

    for load in loads:
        load.wait()
    for c in range(chunks):
        tok_copy(0, c, par, par).wait_recv()
        copy = tok_copy(2, c, par, sib)
        copy.start()
        started.append(copy)
        tok_copy(1, c, sib, sib).wait_recv()
        tok_copy(2, c, dia, sib).wait_recv()
        here = pl.ds(c * CHUNK, CHUNK)
        x = jnp.concatenate([xfull[g, here].astype(jnp.float32) for g in range(n_head)], axis=1)
        square = jnp.sum(x * x, axis=1, keepdims=True) * (1.0 / x.shape[1])
        normed = (x * lax.rsqrt(square + 1e-05) * gain_ref[...]).astype(jnp.bfloat16)
        k = jnp.dot(normed, wk_ref[...], preferred_element_type=jnp.float32)
        v = jnp.dot(normed, wv_ref[...], preferred_element_type=jnp.float32)
        for t in range(n_seq):
            cols = slice(t * HEAD_DIM, (t + 1) * HEAD_DIM)
            kv_out[t, here] = jnp.concatenate([k[:, cols], v[:, cols]], axis=1).astype(jnp.bfloat16)
        for i in range(1, n_seq):
            copy = remote(
                kv_out.at[seq_at[i], here], kv_in.at[s, here],
                kv_send.at[i, c], kv_recv.at[i, c], {"seq": seq_at[i]},
            )
            copy.start()
            started.append(copy)
        kv_in[s, here] = kv_out[s, here]
        q = jnp.dot(normed, wq_ref[...], preferred_element_type=jnp.float32)
        pack = pl.ds(c * HALF, HALF)
        for t in range(n_seq):
            cols = slice(t * HEAD_DIM, (t + 1) * HEAD_DIM)
            q_out[t, pack] = jnp.concatenate([q[:HALF, cols], q[HALF:, cols]], axis=1).astype(jnp.bfloat16)
    for j in range(1, n_head):
        cols = pl.ds(pl.multiple_of(head_at[j] * width, width), width)
        copy = remote(wo_ref.at[:, cols], wo_in.at[h], wo_send.at[j], wo_recv.at[j], {"head": head_at[j]})
        copy.start()
        started.append(copy)
    for j in range(1, n_head):
        remote(
            wo_ref.at[:, pl.ds(0, width)], wo_in.at[head_from[j]], wo_send.at[j], wo_recv.at[j],
            {"head": head_from[j]},
        ).wait_recv()
    for g in range(n_head):
        for t in range(n_seq):
            part = wo_in[g, t * HEAD_DIM:(t + 1) * HEAD_DIM, :]
            at = (g * n_seq + t) * 2 * HEAD_DIM
            w_top[at:at + HEAD_DIM, :] = part
            w_bot[at + HEAD_DIM:at + 2 * HEAD_DIM, :] = part
    for i in range(1, n_seq):
        remote(
            ids_ref.at[seq_from[i]], id_in.at[seq_from[i]], id_send.at[i], id_recv.at[i],
            {"seq": seq_from[i]},
        ).wait_recv()
    for c in range(chunks):
        for i in range(1, n_seq):
            here = pl.ds(c * CHUNK, CHUNK)
            remote(
                kv_out.at[seq_from[i], here], kv_in.at[seq_from[i], here],
                kv_send.at[i, c], kv_recv.at[i, c], {"seq": seq_from[i]},
            ).wait_recv()

    send_queries(n_seq - 1)
    q_in[s] = q_out[s]

    def attend(source, c):
        pair = q_in[source, packed(c)].astype(jnp.float32)
        turned = pltpu.roll(pair, HEAD_DIM, 1)
        query = jnp.concatenate(
            [jnp.where(low, pair, 0.0), jnp.where(low, turned, 0.0)], axis=0
        ).astype(jnp.bfloat16)
        own = jnp.broadcast_to(id_in[source, c, 0:1, :], (CHUNK, CHUNK)).T
        top = None
        for block in range(n_seq * chunks):
            j, e = block // chunks, block % chunks
            kv = kv_in[j, e * CHUNK:(e + 1) * CHUNK, :]
            score = lax.dot_general(query, kv, (((1,), (1,)), ((), ())), preferred_element_type=jnp.float32)
            score = jnp.where(own == id_in[j, e, 0:1, :], score, jnp.float32(-1e30))
            sbuf[:, block * CHUNK:(block + 1) * CHUNK] = score
            peak = jnp.maximum(score[:, :HALF], score[:, HALF:])
            top = peak if top is None else jnp.maximum(top, peak)
        top = jnp.max(top, axis=1, keepdims=True)
        total = None
        acc = None
        for block in range(n_seq * chunks):
            j, e = block // chunks, block % chunks
            kv = kv_in[j, e * CHUNK:(e + 1) * CHUNK, :]
            score = sbuf[:, block * CHUNK:(block + 1) * CHUNK]
            expo = jnp.exp2((score - top) * jnp.float32(LOG2E * HEAD_DIM ** -0.5))
            summed = expo[:, :HALF] + expo[:, HALF:]
            total = summed if total is None else total + summed
            term = jnp.dot(expo.astype(jnp.bfloat16), kv, preferred_element_type=jnp.float32)
            acc = term if acc is None else acc + term
        result = acc / jnp.sum(total, axis=1, keepdims=True)
        return jnp.where(low, pltpu.roll(result[:HALF], HEAD_DIM, 1), result[HALF:]).astype(jnp.bfloat16)

    def ret_copy(i, c, slot, to):
        return remote(
            ret.at[i, packed(c)], back.at[h, slot, packed(c)],
            ret_send.at[i, c], ret_recv.at[i, c], {"seq": to},
        )

    def relay(kind, i, c, owner, to):
        part = back.at[owner, lax.rem(s + n_seq - i, n_seq), packed(c)]
        return remote(part, part, rl_send.at[kind, i, c], rl_recv.at[kind, i, c], {"head": to})

    def pass_on(i, c):
        relay(0, i, c, h, par).start()
        relay(1, i, c, h, sib).start()

    def forward(i, c):
        relay(0, i, c, par, par).wait_recv()
        relay(2, i, c, par, sib).start()

    def back_wait(i, c):
        sender = lax.rem(s + n_seq - i, n_seq)
        ret_copy(i, c, sender, sender).wait_recv()

    lead = chunks - 1
    distant = (n_seq - 1) * chunks
    lag = 2

    @pl.loop(0, n_seq * chunks)
    def _(n):
        r = n - lead
        is_own = (n < lead) | (n == n_seq * chunks - 1)
        i = jnp.where(is_own, 0, (r + chunks) // chunks)
        c = jnp.where(n < lead, n, jnp.where(is_own, chunks - 1, lax.rem(r + chunks, chunks)))
        source = lax.rem(s + i, n_seq)

        for step in range(2, n_seq):
            @pl.when(n == 2 * (step - 2) + 1)
            def _(step=step):
                send_queries(n_seq - step)

        @pl.when(i > 0)
        def _():
            remote(
                q_out.at[source, packed(c)], q_in.at[source, packed(c)],
                q_send.at[n_seq - i, c], q_recv.at[n_seq - i, c], {"seq": source},
            ).wait_recv()

        result = attend(source, c)

        @pl.when(i == 0)
        def _():
            back[h, s, packed(c)] = result
            pass_on(0, c)

        @pl.when(i > 0)
        def _():
            ret[i, packed(c)] = result
            ret_copy(i, c, s, source).start()

        @pl.when((r >= 0) & (r < lead))
        def _():
            forward(0, r)

        @pl.when(r >= lag)
        def _():
            e = r - lag
            back_wait(e // chunks + 1, lax.rem(e, chunks))
            pass_on(e // chunks + 1, lax.rem(e, chunks))

        @pl.when(r >= 2 * lag)
        def _():
            e = r - 2 * lag
            forward(e // chunks + 1, lax.rem(e, chunks))

    for e in range(distant + 1 - lag, distant):
        back_wait(e // chunks + 1, e % chunks)
        pass_on(e // chunks + 1, e % chunks)
    for e in range(distant + 1 - 2 * lag, distant - 1):
        forward(e // chunks + 1, e % chunks)
    forward(0, chunks - 1)
    forward(n_seq - 1, chunks - 1)
    for c in range(chunks):
        for i in range(n_seq):
            relay(1, i, c, sib, sib).wait_recv()
            relay(2, i, c, dia, sib).wait_recv()
        pack = pl.ds(c * HALF, HALF)
        mixed = jnp.concatenate([back[g, t, pack] for g in range(n_head) for t in range(n_seq)], axis=1)
        for weight, at in ((w_top, c * CHUNK), (w_bot, c * CHUNK + HALF)):
            branch = jnp.dot(mixed, weight[...], preferred_element_type=jnp.float32)
            out_ref[at:at + HALF, :] = (xfull[h, at:at + HALF, :].astype(jnp.float32) + branch).astype(jnp.bfloat16)
    for copy in started:
        copy.wait_send()
    for c in range(chunks):
        for i in range(n_seq):
            if i > 0:
                query_copy(i, c).wait_send()
                ret_copy(i, c, s, seq_at[i]).wait_send()
            relay(0, i, c, h, par).wait_send()
            relay(1, i, c, h, sib).wait_send()
            relay(2, i, c, par, sib).wait_send()


def dense(tokens, norm_gain, w_query, w_key, w_value, w_out, cluster_ids):
    n_seq, n_head = lax.axis_size("seq"), lax.axis_size("head")
    tok, width = tokens.shape
    chunks = tok // CHUNK
    ids = cluster_ids[:, :, 0].astype(jnp.float32).reshape(n_seq, chunks, 1, CHUNK)
    ids = jnp.broadcast_to(ids, (n_seq, chunks, 8, CHUNK))
    pair = 2 * HEAD_DIM
    bf16, f32 = jnp.bfloat16, jnp.float32
    vmem, dma = pltpu.VMEM, pltpu.SemaphoreType.DMA
    return pl.pallas_call(
        functools.partial(layer_kernel, n_seq, n_head),
        out_shape=jax.ShapeDtypeStruct((tok, width), bf16),
        in_specs=[pl.BlockSpec(memory_space=pltpu.HBM)] * 7,
        out_specs=pl.BlockSpec(memory_space=pltpu.VMEM),
        scratch_shapes=[
            vmem((1, n_head * width), f32),
            vmem(w_query.shape, bf16), vmem(w_query.shape, bf16), vmem(w_query.shape, bf16),
            dma((7,)),
            vmem((n_head, tok, width), bf16),
            vmem((n_seq, tok, pair), bf16),
            vmem((n_seq, tok, pair), bf16),
            vmem((n_seq, tok // 2, pair), bf16),
            vmem((n_seq, tok // 2, pair), bf16),
            vmem((n_seq, chunks, 8, CHUNK), f32),
            vmem((n_seq, tok // 2, pair), bf16),
            vmem((n_head, n_seq, tok // 2, pair), bf16),
            vmem((n_head, width, width), bf16),
            vmem((n_head * n_seq * pair, width), bf16),
            vmem((n_head * n_seq * pair, width), bf16),
            vmem((CHUNK, n_seq * tok), f32),
            dma((3, chunks)), dma((3, chunks)),
            dma((n_head,)), dma((n_head,)),
            dma((n_seq,)), dma((n_seq,)),
            dma((n_seq, chunks)), dma((n_seq, chunks)),
            dma((n_seq, chunks)), dma((n_seq, chunks)),
            dma((n_seq, chunks)), dma((n_seq, chunks)),
            dma((3, n_seq, chunks)), dma((3, n_seq, chunks)),
        ],
        compiler_params=pltpu.CompilerParams(
            collective_id=0, has_side_effects=True, vmem_limit_bytes=60 * 1024 * 1024
        ),
    )(tokens, norm_gain.reshape(1, -1), w_query, w_key, w_value, w_out, ids)


def on_device(*operands):
    tokens, w_query = operands[0], operands[2]
    n_seq, n_head = lax.axis_size("seq"), lax.axis_size("head")
    heads_here = w_query.shape[1] // HEAD_DIM
    if n_head == 4 and heads_here == n_seq and tokens.shape[0] % CHUNK == 0 and n_seq > 1:
        return dense(*operands)
    return clustered(*operands)


def solution(mesh):
    return jax.shard_map(
        on_device,
        mesh=mesh,
        in_specs=(
            P(("docs", "seq"), "head"),
            P(),
            P(None, "head"),
            P(None, "head"),
            P(None, "head"),
            P("head", None),
            P("head", ("docs", "seq"), None),
        ),
        out_specs=P(("docs", "seq"), "head"),
        check_vma=False,
    )
```

```python
import functools

import jax
import jax.numpy as jnp
from jax import lax
from jax.experimental import pallas as pl
from jax.experimental.pallas import tpu as pltpu
from jax.sharding import PartitionSpec as P

HEAD_DIM = 64
CLUSTERS = 256
CAPACITY = 6


def attend_block(received, marks, n_seq):
    count = received.shape[1]
    span = n_seq * CAPACITY
    parts = received.reshape(3, count, span, HEAD_DIM)
    live = marks.reshape(count, span) > 0.5
    scores = jnp.einsum(
        "csd,ctd->cst", parts[0], parts[1], preferred_element_type=jnp.float32
    ) * HEAD_DIM ** (-0.5)
    scores = jnp.where(live[:, None, :], scores, jnp.float32(-1e30))
    top = jnp.max(scores, axis=-1, keepdims=True)
    expo = jnp.exp(scores - top)
    weights = (expo / jnp.sum(expo, axis=-1, keepdims=True)).astype(jnp.bfloat16)
    result = jnp.einsum(
        "cst,ctd->csd", weights, parts[2], preferred_element_type=jnp.float32
    ).astype(jnp.bfloat16)
    return result.reshape(count, n_seq, CAPACITY * HEAD_DIM)


def place_head(operands):
    head_slot, head_parts = operands
    columns = jnp.arange(CLUSTERS * CAPACITY, dtype=jnp.int32)
    onehot = (head_slot[:, None] == columns[None, :]).astype(jnp.bfloat16)
    placed = jnp.einsum(
        "ts,ctd->csd", onehot, head_parts, preferred_element_type=jnp.float32
    ).astype(jnp.bfloat16)
    filled = jnp.sum(onehot, axis=0, dtype=jnp.float32).astype(jnp.bfloat16)
    return (placed, filled)


def fetch_head(operands):
    head_slot, head_back = operands
    columns = jnp.arange(CLUSTERS * CAPACITY, dtype=jnp.int32)
    onehot = (head_slot[:, None] == columns[None, :]).astype(jnp.bfloat16)
    return jnp.dot(onehot, head_back, preferred_element_type=jnp.float32).astype(jnp.bfloat16)


def clustered(tokens, norm_gain, w_query, w_key, w_value, w_out, cluster_ids):
    n_seq = lax.axis_size("seq")
    tok = tokens.shape[0]
    heads_here = w_query.shape[1] // HEAD_DIM
    owned = CLUSTERS // n_seq
    rows = lax.all_gather(tokens, "head", axis=1, tiled=True)
    inputs = rows.astype(jnp.float32)
    square = jnp.mean(inputs * inputs, axis=-1, keepdims=True)
    normed = (inputs * lax.rsqrt(square + 1e-05) * norm_gain).astype(jnp.bfloat16)
    queries = jnp.dot(normed, w_query, preferred_element_type=jnp.float32).astype(jnp.bfloat16)
    keys = jnp.dot(normed, w_key, preferred_element_type=jnp.float32).astype(jnp.bfloat16)
    values = jnp.dot(normed, w_value, preferred_element_type=jnp.float32).astype(jnp.bfloat16)
    ids = cluster_ids[:, :, 0]
    owner = ids // owned
    within = ids % owned
    positions = jnp.arange(tok, dtype=jnp.int32)
    earlier = positions[None, :] < positions[:, None]
    same = (ids[:, :, None] == ids[:, None, :]) & earlier[None, :, :]
    rank = jnp.sum(same.astype(jnp.int32), axis=2)
    slot_local = (within * n_seq + owner) * CAPACITY + rank
    stacked = jnp.stack([queries, keys, values]).reshape(3, tok, heads_here, HEAD_DIM)
    stacked = stacked.transpose(2, 0, 1, 3)
    placed, filled = lax.map(place_head, (slot_local, stacked))
    outgoing = placed.transpose(1, 0, 2, 3).reshape(
        3, heads_here * owned, n_seq, CAPACITY * HEAD_DIM
    )
    out_marks = filled.reshape(1, heads_here * owned, n_seq, CAPACITY)
    received, in_marks = (
        lax.all_to_all(outgoing, "seq", split_axis=2, concat_axis=2, tiled=True),
        lax.all_to_all(out_marks, "seq", split_axis=2, concat_axis=2, tiled=True),
    )
    result = attend_block(received, in_marks, n_seq)
    returned = lax.all_to_all(result, "seq", split_axis=1, concat_axis=1, tiled=True)
    back_heads = returned.reshape(heads_here, CLUSTERS * CAPACITY, HEAD_DIM)
    fetched = lax.map(fetch_head, (slot_local, back_heads))
    attended = fetched.transpose(1, 0, 2).reshape(tok, heads_here * HEAD_DIM)
    partial_sums = jnp.dot(attended, w_out, preferred_element_type=jnp.float32)
    share = lax.psum_scatter(partial_sums, "head", scatter_dimension=1, tiled=True)
    return (tokens.astype(jnp.float32) + share).astype(jnp.bfloat16)


CHUNK = 256
HALF = CHUNK // 2
MESH = pl.DeviceIdType.MESH
LOG2E = 1.4426950408889634


def remote(src, dst, send, recv, where):
    return pltpu.make_async_remote_copy(
        src_ref=src, dst_ref=dst, send_sem=send, recv_sem=recv, device_id=where, device_id_type=MESH
    )


def layer_kernel(
    n_seq, n_head, tok_ref, gain_hbm, wq_hbm, wk_hbm, wv_hbm, wo_ref, ids_ref, out_ref,
    gain_ref, wq_ref, wk_ref, wv_ref, load_sem,
    xfull, kv_out, kv_in, q_out, q_in, id_in, ret, back, wo_in, w_top, w_bot, sbuf,
    tok_send, tok_recv, wo_send, wo_recv, id_send, id_recv, kv_send, kv_recv,
    q_send, q_recv, ret_send, ret_recv, rl_send, rl_recv,
):
    s = lax.axis_index("seq")
    h = lax.axis_index("head")
    tok, width = tok_ref.shape
    chunks = tok // CHUNK
    sib = h + 1 - 2 * lax.rem(h, 2)
    par = lax.rem(h + 2, 4)
    dia = lax.rem(sib + 2, 4)
    seq_at = [lax.rem(s + i, n_seq) for i in range(n_seq)]
    seq_from = [lax.rem(s + n_seq - i, n_seq) for i in range(n_seq)]
    head_at = [lax.rem(h + j, n_head) for j in range(n_head)]
    head_from = [lax.rem(h + n_head - j, n_head) for j in range(n_head)]

    own_cols = pl.ds(pl.multiple_of(h * width, width), width)
    loads = [
        pltpu.make_async_copy(src, dst, load_sem.at[n])
        for n, (src, dst) in enumerate((
            (tok_ref, xfull.at[h]), (gain_hbm, gain_ref), (wk_hbm, wk_ref), (wv_hbm, wv_ref), (wq_hbm, wq_ref),
            (wo_ref.at[:, own_cols], wo_in.at[h]), (ids_ref.at[s], id_in.at[s]),
        ))
    ]
    for load in loads:
        load.start()
    barrier = pltpu.get_barrier_semaphore()
    for i in range(1, n_seq):
        pl.semaphore_signal(barrier, inc=1, device_id={"seq": seq_at[i]}, device_id_type=MESH)
    for j in range(1, n_head):
        pl.semaphore_signal(barrier, inc=1, device_id={"head": head_at[j]}, device_id_type=MESH)
    pl.semaphore_wait(barrier, n_seq + n_head - 2)

    def rows(c):
        return pl.ds(pl.multiple_of(c * CHUNK, CHUNK), CHUNK)

    def packed(c):
        return pl.ds(pl.multiple_of(c * HALF, HALF), HALF)

    started = []

    def tok_copy(kind, c, owner, to):
        src = tok_ref.at[rows(c)] if kind < 2 else xfull.at[owner, rows(c)]
        return remote(src, xfull.at[owner, rows(c)], tok_send.at[kind, c], tok_recv.at[kind, c], {"head": to})

    for c in range(chunks):
        for kind, to in ((0, par), (1, sib)):
            copy = tok_copy(kind, c, h, to)
            copy.start()
            started.append(copy)
    for i in range(1, n_seq):
        copy = remote(ids_ref.at[seq_at[i]], id_in.at[s], id_send.at[i], id_recv.at[i], {"seq": seq_at[i]})
        copy.start()
        started.append(copy)
    w_top[...] = jnp.zeros_like(w_top)
    w_bot[...] = jnp.zeros_like(w_bot)

    def query_copy(i, c):
        return remote(
            q_out.at[lax.rem(s + i, n_seq), packed(c)], q_in.at[s, packed(c)],
            q_send.at[i, c], q_recv.at[i, c], {"seq": lax.rem(s + i, n_seq)},
        )

    def send_queries(i):
        for c in range(chunks):
            query_copy(i, c).start()

    lane = lax.broadcasted_iota(jnp.int32, (HALF, 2 * HEAD_DIM), 1)
    low = lane < HEAD_DIM

    for load in loads:
        load.wait()
    for c in range(chunks):
        tok_copy(0, c, par, par).wait_recv()
        copy = tok_copy(2, c, par, sib)
        copy.start()
        started.append(copy)
        tok_copy(1, c, sib, sib).wait_recv()
        tok_copy(2, c, dia, sib).wait_recv()
        here = pl.ds(c * CHUNK, CHUNK)
        x = jnp.concatenate([xfull[g, here].astype(jnp.float32) for g in range(n_head)], axis=1)
        square = jnp.sum(x * x, axis=1, keepdims=True) * (1.0 / x.shape[1])
        normed = (x * lax.rsqrt(square + 1e-05) * gain_ref[...]).astype(jnp.bfloat16)
        k = jnp.dot(normed, wk_ref[...], preferred_element_type=jnp.float32)
        v = jnp.dot(normed, wv_ref[...], preferred_element_type=jnp.float32)
        for t in range(n_seq):
            cols = slice(t * HEAD_DIM, (t + 1) * HEAD_DIM)
            kv_out[t, here] = jnp.concatenate([k[:, cols], v[:, cols]], axis=1).astype(jnp.bfloat16)
        for i in range(1, n_seq):
            copy = remote(
                kv_out.at[seq_at[i], here], kv_in.at[s, here],
                kv_send.at[i, c], kv_recv.at[i, c], {"seq": seq_at[i]},
            )
            copy.start()
            started.append(copy)
        kv_in[s, here] = kv_out[s, here]
        q = jnp.dot(normed, wq_ref[...], preferred_element_type=jnp.float32)
        pack = pl.ds(c * HALF, HALF)
        for t in range(n_seq):
            cols = slice(t * HEAD_DIM, (t + 1) * HEAD_DIM)
            q_out[t, pack] = jnp.concatenate([q[:HALF, cols], q[HALF:, cols]], axis=1).astype(jnp.bfloat16)
    for j in range(1, n_head):
        cols = pl.ds(pl.multiple_of(head_at[j] * width, width), width)
        copy = remote(wo_ref.at[:, cols], wo_in.at[h], wo_send.at[j], wo_recv.at[j], {"head": head_at[j]})
        copy.start()
        started.append(copy)
    for j in range(1, n_head):
        remote(
            wo_ref.at[:, pl.ds(0, width)], wo_in.at[head_from[j]], wo_send.at[j], wo_recv.at[j],
            {"head": head_from[j]},
        ).wait_recv()
    for g in range(n_head):
        for t in range(n_seq):
            part = wo_in[g, t * HEAD_DIM:(t + 1) * HEAD_DIM, :]
            at = (g * n_seq + t) * 2 * HEAD_DIM
            w_top[at:at + HEAD_DIM, :] = part
            w_bot[at + HEAD_DIM:at + 2 * HEAD_DIM, :] = part
    for i in range(1, n_seq):
        remote(
            ids_ref.at[seq_from[i]], id_in.at[seq_from[i]], id_send.at[i], id_recv.at[i],
            {"seq": seq_from[i]},
        ).wait_recv()
    for c in range(chunks):
        for i in range(1, n_seq):
            here = pl.ds(c * CHUNK, CHUNK)
            remote(
                kv_out.at[seq_from[i], here], kv_in.at[seq_from[i], here],
                kv_send.at[i, c], kv_recv.at[i, c], {"seq": seq_from[i]},
            ).wait_recv()

    send_queries(n_seq - 1)
    q_in[s] = q_out[s]

    def attend(source, c):
        pair = q_in[source, packed(c)].astype(jnp.float32)
        turned = pltpu.roll(pair, HEAD_DIM, 1)
        query = jnp.concatenate(
            [jnp.where(low, pair, 0.0), jnp.where(low, turned, 0.0)], axis=0
        ).astype(jnp.bfloat16)
        own = jnp.broadcast_to(id_in[source, c, 0:1, :], (CHUNK, CHUNK)).T
        top = None
        for block in range(n_seq * chunks):
            j, e = block // chunks, block % chunks
            kv = kv_in[j, e * CHUNK:(e + 1) * CHUNK, :]
            score = lax.dot_general(query, kv, (((1,), (1,)), ((), ())), preferred_element_type=jnp.float32)
            score = jnp.where(own == id_in[j, e, 0:1, :], score, jnp.float32(-1e30))
            sbuf[:, block * CHUNK:(block + 1) * CHUNK] = score
            peak = jnp.maximum(score[:, :HALF], score[:, HALF:])
            top = peak if top is None else jnp.maximum(top, peak)
        top = jnp.max(top, axis=1, keepdims=True)
        total = None
        acc = None
        for block in range(n_seq * chunks):
            j, e = block // chunks, block % chunks
            kv = kv_in[j, e * CHUNK:(e + 1) * CHUNK, :]
            score = sbuf[:, block * CHUNK:(block + 1) * CHUNK]
            expo = jnp.exp2((score - top) * jnp.float32(LOG2E * HEAD_DIM ** -0.5))
            summed = expo[:, :HALF] + expo[:, HALF:]
            total = summed if total is None else total + summed
            term = jnp.dot(expo.astype(jnp.bfloat16), kv, preferred_element_type=jnp.float32)
            acc = term if acc is None else acc + term
        result = acc / jnp.sum(total, axis=1, keepdims=True)
        return jnp.where(low, pltpu.roll(result[:HALF], HEAD_DIM, 1), result[HALF:]).astype(jnp.bfloat16)

    def ret_copy(i, c, slot, to):
        return remote(
            ret.at[i, packed(c)], back.at[h, slot, packed(c)],
            ret_send.at[i, c], ret_recv.at[i, c], {"seq": to},
        )

    def relay(kind, i, c, owner, to):
        part = back.at[owner, lax.rem(s + n_seq - i, n_seq), packed(c)]
        return remote(part, part, rl_send.at[kind, i, c], rl_recv.at[kind, i, c], {"head": to})

    def pass_on(i, c):
        relay(0, i, c, h, par).start()
        relay(1, i, c, h, sib).start()

    def forward(i, c):
        relay(0, i, c, par, par).wait_recv()
        relay(2, i, c, par, sib).start()

    def back_wait(i, c):
        sender = lax.rem(s + n_seq - i, n_seq)
        ret_copy(i, c, sender, sender).wait_recv()

    lead = chunks - 1
    distant = (n_seq - 1) * chunks
    lag = 3

    @pl.loop(0, n_seq * chunks)
    def _(n):
        r = n - lead
        is_own = (n < lead) | (n == n_seq * chunks - 1)
        i = jnp.where(is_own, 0, (r + chunks) // chunks)
        c = jnp.where(n < lead, n, jnp.where(is_own, chunks - 1, lax.rem(r + chunks, chunks)))
        source = lax.rem(s + i, n_seq)

        for step in range(2, n_seq):
            @pl.when(n == 2 * (step - 2) + 1)
            def _(step=step):
                send_queries(n_seq - step)

        @pl.when(i > 0)
        def _():
            remote(
                q_out.at[source, packed(c)], q_in.at[source, packed(c)],
                q_send.at[n_seq - i, c], q_recv.at[n_seq - i, c], {"seq": source},
            ).wait_recv()

        result = attend(source, c)

        @pl.when(i == 0)
        def _():
            back[h, s, packed(c)] = result
            pass_on(0, c)

        @pl.when(i > 0)
        def _():
            ret[i, packed(c)] = result
            ret_copy(i, c, s, source).start()

        @pl.when((r >= 0) & (r < lead))
        def _():
            forward(0, r)

        @pl.when(r >= lag)
        def _():
            e = r - lag
            back_wait(e // chunks + 1, lax.rem(e, chunks))
            pass_on(e // chunks + 1, lax.rem(e, chunks))

        @pl.when(r >= 2 * lag)
        def _():
            e = r - 2 * lag
            forward(e // chunks + 1, lax.rem(e, chunks))

    for e in range(distant + 1 - lag, distant):
        back_wait(e // chunks + 1, e % chunks)
        pass_on(e // chunks + 1, e % chunks)
    for e in range(distant + 1 - 2 * lag, distant - 1):
        forward(e // chunks + 1, e % chunks)
    forward(0, chunks - 1)
    forward(n_seq - 1, chunks - 1)
    for c in range(chunks):
        for i in range(n_seq):
            relay(1, i, c, sib, sib).wait_recv()
            relay(2, i, c, dia, sib).wait_recv()
        pack = pl.ds(c * HALF, HALF)
        mixed = jnp.concatenate([back[g, t, pack] for g in range(n_head) for t in range(n_seq)], axis=1)
        for weight, at in ((w_top, c * CHUNK), (w_bot, c * CHUNK + HALF)):
            branch = jnp.dot(mixed, weight[...], preferred_element_type=jnp.float32)
            out_ref[at:at + HALF, :] = (xfull[h, at:at + HALF, :].astype(jnp.float32) + branch).astype(jnp.bfloat16)
    for copy in started:
        copy.wait_send()
    for c in range(chunks):
        for i in range(n_seq):
            if i > 0:
                query_copy(i, c).wait_send()
                ret_copy(i, c, s, seq_at[i]).wait_send()
            relay(0, i, c, h, par).wait_send()
            relay(1, i, c, h, sib).wait_send()
            relay(2, i, c, par, sib).wait_send()


def dense(tokens, norm_gain, w_query, w_key, w_value, w_out, cluster_ids):
    n_seq, n_head = lax.axis_size("seq"), lax.axis_size("head")
    tok, width = tokens.shape
    chunks = tok // CHUNK
    ids = cluster_ids[:, :, 0].astype(jnp.float32).reshape(n_seq, chunks, 1, CHUNK)
    ids = jnp.broadcast_to(ids, (n_seq, chunks, 8, CHUNK))
    pair = 2 * HEAD_DIM
    bf16, f32 = jnp.bfloat16, jnp.float32
    vmem, dma = pltpu.VMEM, pltpu.SemaphoreType.DMA
    return pl.pallas_call(
        functools.partial(layer_kernel, n_seq, n_head),
        out_shape=jax.ShapeDtypeStruct((tok, width), bf16),
        in_specs=[pl.BlockSpec(memory_space=pltpu.HBM)] * 7,
        out_specs=pl.BlockSpec(memory_space=pltpu.VMEM),
        scratch_shapes=[
            vmem((1, n_head * width), f32),
            vmem(w_query.shape, bf16), vmem(w_query.shape, bf16), vmem(w_query.shape, bf16),
            dma((7,)),
            vmem((n_head, tok, width), bf16),
            vmem((n_seq, tok, pair), bf16),
            vmem((n_seq, tok, pair), bf16),
            vmem((n_seq, tok // 2, pair), bf16),
            vmem((n_seq, tok // 2, pair), bf16),
            vmem((n_seq, chunks, 8, CHUNK), f32),
            vmem((n_seq, tok // 2, pair), bf16),
            vmem((n_head, n_seq, tok // 2, pair), bf16),
            vmem((n_head, width, width), bf16),
            vmem((n_head * n_seq * pair, width), bf16),
            vmem((n_head * n_seq * pair, width), bf16),
            vmem((CHUNK, n_seq * tok), f32),
            dma((3, chunks)), dma((3, chunks)),
            dma((n_head,)), dma((n_head,)),
            dma((n_seq,)), dma((n_seq,)),
            dma((n_seq, chunks)), dma((n_seq, chunks)),
            dma((n_seq, chunks)), dma((n_seq, chunks)),
            dma((n_seq, chunks)), dma((n_seq, chunks)),
            dma((3, n_seq, chunks)), dma((3, n_seq, chunks)),
        ],
        compiler_params=pltpu.CompilerParams(
            collective_id=0, has_side_effects=True, vmem_limit_bytes=60 * 1024 * 1024
        ),
    )(tokens, norm_gain.reshape(1, -1), w_query, w_key, w_value, w_out, ids)


def on_device(*operands):
    tokens, w_query = operands[0], operands[2]
    n_seq, n_head = lax.axis_size("seq"), lax.axis_size("head")
    heads_here = w_query.shape[1] // HEAD_DIM
    if n_head == 4 and heads_here == n_seq and tokens.shape[0] % CHUNK == 0 and n_seq > 1:
        return dense(*operands)
    return clustered(*operands)


def solution(mesh):
    return jax.shard_map(
        on_device,
        mesh=mesh,
        in_specs=(
            P(("docs", "seq"), "head"),
            P(),
            P(None, "head"),
            P(None, "head"),
            P(None, "head"),
            P("head", None),
            P("head", ("docs", "seq"), None),
        ),
        out_specs=P(("docs", "seq"), "head"),
        check_vma=False,
    )
```
